256 devices in a mesh: seq: 64 (over y, z_hi, x), head: 4 (over z_lo, core).
Axes of the slice: x: 4, y: 4, z: 8 (z_hi: 4, z_lo: 2; z = z_hi * 2 + z_lo), core: 2. Of those that a mesh axis runs over, the one named last changes fastest.
Arguments:
- hidden: bfloat16 [32768, 5120], P('seq'), may hold values from -6 to 6
- w_query: bfloat16 [5120, 512], P(None, 'head')
- w_key: bfloat16 [5120, 512], P(None, 'head')
- w_value: bfloat16 [5120, 512], P(None, 'head'), may hold values from -0.078125 to 0.078125
- w_out: bfloat16 [512, 5120], replicated, may hold values from -1 to 1
- valid: int32 [32768], P('seq'), may hold values from 0 to 1, as said below
- window: int32 [10], replicated, may hold values from 0 to 20, as said below
- frame_ids: int32 [32768], P('seq'), may hold values from 0 to 22, as said below
Outputs:
- mixed: bfloat16 [32768, 5120], P(('seq', 'head'))
The draws below stay inside these ranges and needn't reach their ends.
Inputs may be any that keep to these rules, and one draw needn't show every extreme that they name: valid[t] = 1 exactly where frame_ids[t] <= 21. `frame_ids`: every frame 0 to 21 has exactly 1466 tokens, contiguous; padding lies in gaps between or around frames. `window`: distinct, increasing, always holding frames 0 and 20; so exactly 14660 tokens are queries.
All inputs are finite; a program needn't handle non-finite values.
Results may differ from the reference program's by a relative error of at most 0.015.
Values may be sent and summed in bfloat16 or wider, within the bound.
No kernel may reach another device: no remote copies, remote signals or barrier semaphores. Data moves between devices by JAX's collectives and lax.ppermute only.
A program may use at most 192 MiB of HBM per device.

```python
import math
import jax
import jax.numpy as jnp
from jax import lax

D = 5120
HD = 128
FRAMES = 21
WINDOW = 10
TOKENS = 32768
FRAME_TOK = 1466
HEADS = 4


def layout(key):
    pads = TOKENS - (FRAMES + 1) * FRAME_TOK
    cuts = jnp.sort(jax.random.randint(jax.random.fold_in(key, 101), (FRAMES + 1,), 0, pads + 1))
    starts = jnp.arange(FRAMES + 1, dtype=jnp.int32) * FRAME_TOK + cuts.astype(jnp.int32)
    place = jnp.arange(TOKENS, dtype=jnp.int32)
    segment = jnp.sum((place[:, None] >= starts[None, :]).astype(jnp.int32), axis=1) - 1
    begin = jnp.take(starts, jnp.maximum(segment, 0))
    inside = (segment >= 0) & (place - begin < FRAME_TOK)
    ref_slot = jax.random.randint(jax.random.fold_in(key, 102), (), 0, FRAMES + 1)
    frame = jnp.where(segment < ref_slot, segment, jnp.where(segment == ref_slot, FRAMES, segment - 1))
    frame = jnp.where(inside, frame, FRAMES + 1)
    return (frame.astype(jnp.int32), inside.astype(jnp.int32))


def draw_valid(key, part):
    return layout(key)[1]


def draw_frame_ids(key, part):
    return layout(key)[0]


def draw_window(key, part):
    key = jax.random.fold_in(key, 7)
    middle = jax.random.permutation(key, FRAMES - 2)[:WINDOW - 2].astype(jnp.int32) + 1
    first = jnp.zeros((1,), jnp.int32)
    last = jnp.full((1,), FRAMES - 1, jnp.int32)
    return jnp.sort(jnp.concatenate([first, middle, last])).astype(jnp.int32)


def draw_hidden(key, part):
    key = jax.random.fold_in(key, 3)
    return jnp.clip(jax.random.normal(key, (TOKENS, D), jnp.float32), -6.0, 6.0).astype(jnp.bfloat16)


def shared_base(key):
    return jnp.clip(jax.random.normal(key, (D, HEADS * HD), jnp.float32), -6.0, 6.0)


def draw_w_query(key, part):
    base = shared_base(key)
    return (base * (2.0 / math.sqrt(D))).astype(jnp.bfloat16)


def draw_w_key(key, part):
    key = jax.random.fold_in(key, 5)
    own = jnp.clip(jax.random.normal(key, (D, HEADS * HD), jnp.float32), -6.0, 6.0)
    mixed = own
    return (mixed / math.sqrt(D)).astype(jnp.bfloat16)


def block_levels(key, shape, pieces, low, top_value):
    loudness = 1.0
    for dim, parts in pieces:
        heights = jax.random.uniform(jax.random.fold_in(jax.random.fold_in(key, 6), dim), (parts,), jnp.float32, low / len(pieces), top_value / len(pieces))
        loudness = loudness * jnp.repeat(jnp.exp(heights), shape[dim] // parts).reshape((-1,) + (1,) * (len(shape) - 1 - dim))
    return loudness


def normal_values(own_key, dims, scale, bound, shards=(), kind=jnp.bfloat16):
    values = scale * jax.random.normal(own_key, dims, jnp.float32)
    if shards:
        values = values * block_levels(own_key, dims, shards, -0.22, 0.18)
    return jnp.clip(values, -bound, bound).astype(kind)


def setup_inputs(seed: int = 0) -> dict:
    key_list = jax.random.split(jax.random.key(seed), 9)
    hidden = draw_hidden(jax.random.fold_in(key_list[8], 71), 0)
    w_query = draw_w_query(jax.random.fold_in(key_list[8], 71), 0)
    w_key = draw_w_key(jax.random.fold_in(key_list[8], 71), 0)
    w_value = normal_values(key_list[3], (D, HEADS * HD), D ** -0.5, 0.078125, ((1, 4),))
    w_out = normal_values(key_list[4], (HEADS * HD, D), (HEADS * 8) ** -0.5, 1.0)
    valid = draw_valid(jax.random.fold_in(key_list[8], 71), 0)
    window = draw_window(jax.random.fold_in(key_list[8], 71), 0)
    frame_ids = draw_frame_ids(jax.random.fold_in(key_list[8], 71), 0)
    return dict(hidden=hidden, w_query=w_query, w_key=w_key, w_value=w_value, w_out=w_out, valid=valid, window=window, frame_ids=frame_ids)


def reference(hidden, w_query, w_key, w_value, w_out, valid, window, frame_ids):
    queries = jnp.dot(hidden, w_query, preferred_element_type=jnp.float32).astype(jnp.bfloat16)
    keys = jnp.dot(hidden, w_key, preferred_element_type=jnp.float32).astype(jnp.bfloat16)
    values = jnp.dot(hidden, w_value, preferred_element_type=jnp.float32).astype(jnp.bfloat16)
    chosen = jnp.any(frame_ids[:, None] == window[None, :], axis=1) & (valid > 0)
    count = WINDOW * FRAME_TOK
    padded = (count + 511) // 512 * 512
    picked = jnp.nonzero(chosen, size=padded, fill_value=TOKENS)[0].astype(jnp.int32)
    safe_rows = jnp.minimum(picked, TOKENS - 1)
    scale = 1.0 / math.sqrt(HD)
    live = valid > 0
    outputs = []
    for head in range(HEADS):
        k_head = keys[:, head * HD:(head + 1) * HD]
        v_head = values[:, head * HD:(head + 1) * HD]
        q_rows = jnp.take(queries[:, head * HD:(head + 1) * HD], safe_rows, axis=0).reshape(padded // 512, 512, HD)

        def attend(block):
            scores = jnp.dot(block, k_head.T, preferred_element_type=jnp.float32) * scale
            scores = jnp.where(live[None, :], scores, -1e+30)
            peak = lax.optimization_barrier(jnp.max(scores, axis=1, keepdims=True))
            weights = jnp.exp(scores - peak)
            numer = jnp.dot(weights.astype(jnp.bfloat16), v_head, preferred_element_type=jnp.float32)
            return (numer / lax.optimization_barrier(jnp.sum(weights, axis=1, keepdims=True))).astype(jnp.bfloat16)
        outputs.append(lax.map(attend, q_rows).reshape(padded, HD))
    result = jnp.concatenate(outputs, axis=1)
    attended = jnp.zeros((TOKENS, HEADS * HD), jnp.bfloat16).at[picked].set(result, mode='drop')
    return jnp.dot(attended, w_out, preferred_element_type=jnp.float32).astype(jnp.bfloat16)
```

```python
import math

import jax
import jax.numpy as jnp
from jax import lax
from jax.experimental import pallas as pl
from jax.experimental.pallas import tpu as pltpu
from jax.sharding import Mesh, PartitionSpec as P

HD = 128
TOK = 512
QUARTER = 128
ROWS = 144
FLAG = 2.0 ** 100
LOW = -1e30
NT = (((1,), (1,)), ((), ()))
VMEM_LIMIT = 56 * 2 ** 20


def eye():
    return lax.broadcasted_iota(jnp.int32, (128, 128), 0) == lax.broadcasted_iota(jnp.int32, (128, 128), 1)


def to_column(row):
    return jnp.sum(jnp.where(eye(), jnp.broadcast_to(row, (128, 128)), 0.0), axis=1, keepdims=True)


def to_row(column):
    return jnp.sum(jnp.where(eye(), jnp.broadcast_to(column, (128, 128)), 0.0), axis=0, keepdims=True)


def project_kernel(hid, wq, wk, wv, valid, q_ref, kv_ref, acc_q, acc_kv):
    step = pl.program_id(0)

    @pl.when(step == 0)
    def _():
        acc_q[...] = jnp.zeros_like(acc_q)
        acc_kv[...] = jnp.zeros_like(acc_kv)

    rows = hid[...]
    w = jnp.concatenate([wk[...], wv[...]], axis=1)
    acc_kv[...] += jnp.dot(rows, w, preferred_element_type=jnp.float32)
    acc_q[...] += jnp.dot(rows, wq[...], preferred_element_type=jnp.float32)

    @pl.when(step == pl.num_programs(0) - 1)
    def _():
        q_ref[...] = (acc_q[...] * (math.log2(math.e) / math.sqrt(HD))).astype(jnp.bfloat16)
        kv_ref[:, :HD] = acc_kv[:, :HD].astype(jnp.bfloat16)
        for i in range(TOK // 128):
            live = to_column(valid[i:i + 1, :].astype(jnp.float32))
            part = acc_kv[i * 128:(i + 1) * 128, HD:]
            kv_ref[i * 128:(i + 1) * 128, HD:] = jnp.where(live > 0.5, part, FLAG).astype(jnp.bfloat16)


def project(hidden, wq, wk, wv, valid):
    depth = hidden.shape[1]
    size = 512
    return pl.pallas_call(
        project_kernel,
        grid=(depth // size,),
        in_specs=[
            pl.BlockSpec((TOK, size), lambda k: (0, k)),
            pl.BlockSpec((size, HD), lambda k: (k, 0)),
            pl.BlockSpec((size, HD), lambda k: (k, 0)),
            pl.BlockSpec((size, HD), lambda k: (k, 0)),
            pl.BlockSpec((4, 128), lambda k: (0, 0)),
        ],
        out_specs=[
            pl.BlockSpec((TOK, HD), lambda k: (0, 0)),
            pl.BlockSpec((TOK, 2 * HD), lambda k: (0, 0)),
        ],
        out_shape=[
            jax.ShapeDtypeStruct((TOK, HD), jnp.bfloat16),
            jax.ShapeDtypeStruct((TOK, 2 * HD), jnp.bfloat16),
        ],
        scratch_shapes=[pltpu.VMEM((TOK, HD), jnp.float32), pltpu.VMEM((TOK, 2 * HD), jnp.float32)],
        compiler_params=pltpu.CompilerParams(vmem_limit_bytes=VMEM_LIMIT),
        cost_estimate=pl.CostEstimate(flops=2 * TOK * depth * 3 * HD, bytes_accessed=10_000_000, transcendentals=0),
        name="project",
    )(hidden, wq, wk, wv, valid.reshape(4, 128))


def attend_kernel(n_q, n_kv, chunk, first, last, *refs):
    place = refs[0]
    q_refs = refs[1:1 + n_q]
    kv_refs = refs[1 + n_q:1 + n_q + n_kv]
    rest = refs[1 + n_q + n_kv:]
    if first:
        state_in = None
    else:
        state_in, rest = rest[0], rest[1:]
    out, kx, vx, qx = rest
    start = 0
    for ref in kv_refs:
        size = ref.shape[0]
        lane = lax.broadcasted_iota(jnp.int32, (size, HD), 1)
        vals = ref[:, HD:].astype(jnp.float32)
        live = vals[:, :1] < FLAG * 0.5
        kx[start:start + size, :HD] = ref[:, :HD]
        kx[start:start + size, HD:] = jnp.where((~live) & (lane == 0), LOW, 0.0).astype(jnp.bfloat16)
        vx[start:start + size, :HD] = jnp.where(live, vals, 0.0).astype(jnp.bfloat16)
        vx[start:start + size, HD:] = jnp.where(live & (lane == 0), 1.0, 0.0).astype(jnp.bfloat16)
        start += size
    total = start
    lane = lax.broadcasted_iota(jnp.int32, (TOK, HD), 1)
    one = jnp.where(lane == 0, 1.0, 0.0).astype(jnp.bfloat16)
    for i, ref in enumerate(q_refs):
        qx[i, :, :HD] = ref[...]
        qx[i, :, HD:] = one
    wide = lax.broadcasted_iota(jnp.int32, (TOK, 2 * HD), 1)

    def block(i, carry):
        q = qx[i]

        def score(j):
            return lax.dot_general(q, kx[j * chunk:(j + 1) * chunk, :], NT, preferred_element_type=jnp.float32)

        if first:
            peak = jnp.full((TOK, 1), LOW, jnp.float32)
            acc = jnp.zeros((TOK, 2 * HD), jnp.float32)
        else:
            acc = state_in[i]
            peak = acc[:, HD + 1:HD + 2]
        steps = total // chunk
        s = score(0)
        for j in range(steps):
            ahead = score(j + 1) if j + 1 < steps else None
            new_peak = jnp.maximum(peak, jnp.max(s, axis=1, keepdims=True))
            factor = jnp.exp2(peak - new_peak)
            weights = jnp.exp2(s - new_peak).astype(jnp.bfloat16)
            acc = acc * factor + jnp.dot(weights, vx[j * chunk:(j + 1) * chunk, :], preferred_element_type=jnp.float32)
            peak = new_peak
            s = ahead
        if not last:
            out[i] = jnp.where(wide == HD + 1, peak, acc)
        else:
            mass = acc[:, HD:HD + 1]
            result = (acc[:, :HD] / mass).astype(jnp.bfloat16)
            logs = peak + jnp.log2(mass)
            home = lax.rem(place[0] - i + 4, 4)
            for k in range(4):
                out[home * 4 + k, :QUARTER, :] = result[k * QUARTER:(k + 1) * QUARTER, :]
                row = to_row(logs[k * QUARTER:(k + 1) * QUARTER, :])
                high = row.astype(jnp.bfloat16).astype(jnp.float32)
                mid = (row - high).astype(jnp.bfloat16).astype(jnp.float32)
                low = row - high - mid
                sub = lax.broadcasted_iota(jnp.int32, (ROWS - QUARTER, 128), 0)
                tile = jnp.where(sub == 0, high, jnp.where(sub == 1, mid, jnp.where(sub == 2, low, 0.0)))
                out[home * 4 + k, QUARTER:, :] = tile.astype(jnp.bfloat16)
        return carry

    lax.fori_loop(0, n_q, block, 0)


def attend(place, queries, pieces, state, chunk, last):
    total = sum(p.shape[0] for p in pieces)
    n_q = len(queries)
    first = state is None
    if last:
        out = jax.ShapeDtypeStruct((4 * n_q, ROWS, HD), jnp.bfloat16)
    else:
        out = jax.ShapeDtypeStruct((n_q, TOK, 2 * HD), jnp.float32)
    args = [place] + list(queries) + list(pieces) + ([] if first else [state])
    body = lambda *refs: attend_kernel(n_q, len(pieces), chunk, first, last, *refs)
    return pl.pallas_call(
        body,
        in_specs=[pl.BlockSpec(memory_space=pltpu.SMEM)] + [pl.BlockSpec(memory_space=pltpu.VMEM)] * (len(args) - 1),
        out_specs=pl.BlockSpec(memory_space=pltpu.VMEM),
        out_shape=out,
        scratch_shapes=[
            pltpu.VMEM((total, 2 * HD), jnp.bfloat16),
            pltpu.VMEM((total, 2 * HD), jnp.bfloat16),
            pltpu.VMEM((n_q, TOK, 2 * HD), jnp.bfloat16),
        ],
        compiler_params=pltpu.CompilerParams(vmem_limit_bytes=VMEM_LIMIT),
        cost_estimate=pl.CostEstimate(
            flops=8 * n_q * TOK * total * HD, bytes_accessed=total * 512 + n_q * TOK * 1024, transcendentals=n_q * TOK * total),
        name="attend",
    )(*args)


def finish_kernel(parts, chosen, w, out, mixed):
    @pl.when(pl.program_id(0) == 0)
    def _():
        picked = to_column(chosen[...].astype(jnp.float32)) > 0.5
        for h in range(4):
            logs = []
            for r in range(4):
                tile = parts[r * 4 + h, QUARTER:, :].astype(jnp.float32)
                logs.append(tile[0:1, :] + tile[1:2, :] + tile[2:3, :])
            top = jnp.maximum(jnp.maximum(logs[0], logs[1]), jnp.maximum(logs[2], logs[3]))
            shares = [jnp.exp2(x - top) for x in logs]
            whole = shares[0] + shares[1] + shares[2] + shares[3]
            acc = jnp.zeros((QUARTER, HD), jnp.float32)
            for r in range(4):
                acc += to_column(shares[r] / whole) * parts[r * 4 + h, :QUARTER, :].astype(jnp.float32)
            mixed[:, h * HD:(h + 1) * HD] = jnp.where(picked, acc, 0.0).astype(jnp.bfloat16)

    out[...] = jnp.dot(mixed[...], w[...], preferred_element_type=jnp.float32).astype(jnp.bfloat16)


def finish(parts, chosen, w_out):
    width = w_out.shape[1]
    size = 1024
    return pl.pallas_call(
        finish_kernel,
        grid=(width // size,),
        in_specs=[
            pl.BlockSpec((16, ROWS, HD), lambda j: (0, 0, 0)),
            pl.BlockSpec((1, QUARTER), lambda j: (0, 0)),
            pl.BlockSpec((4 * HD, size), lambda j: (0, j)),
        ],
        out_specs=pl.BlockSpec((QUARTER, size), lambda j: (0, j)),
        out_shape=jax.ShapeDtypeStruct((QUARTER, width), jnp.bfloat16),
        scratch_shapes=[pltpu.VMEM((QUARTER, 4 * HD), jnp.bfloat16)],
        compiler_params=pltpu.CompilerParams(vmem_limit_bytes=VMEM_LIMIT),
        cost_estimate=pl.CostEstimate(flops=2 * QUARTER * 4 * HD * width, bytes_accessed=7_000_000, transcendentals=0),
        name="finish",
    )(parts, chosen, w_out)


def shift(x, axis, by):
    return lax.ppermute(x, axis, [(i, (i + by) % 4) for i in range(4)])


def body(hidden, w_query, w_key, w_value, w_out, valid, window, frame_ids):
    chosen = jnp.any(frame_ids[:, None] == window[None, :], axis=1) & (valid > 0)
    quarter = lax.axis_index("head")
    mine = lax.dynamic_slice(chosen.astype(jnp.int32), (quarter * QUARTER,), (QUARTER,)).reshape(1, QUARTER)
    place = lax.axis_index("zh").astype(jnp.int32).reshape(1)
    q, kv = project(hidden, w_query, w_key, w_value, valid)
    half = TOK // 2
    along_x = {s: shift(kv, "x", s) for s in (1, 3, 2)}
    along_y = {s: shift(kv, "y", s) for s in (1, 3, 2)}
    queries = [q] + [shift(q, "zh", s) for s in (1, 2, 3)]
    state = attend(
        place, queries, [kv] + [along_x[s] for s in (1, 2, 3)] + [along_y[s] for s in (1, 2, 3)], None, 1792, False)
    from_x = jnp.concatenate([along_x[s][:half] for s in (1, 2, 3)], axis=0)
    from_y = jnp.concatenate([along_y[s][half:] for s in (1, 2, 3)], axis=0)
    pieces = []
    for s in (1, 3, 2):
        pieces.append(shift(from_x, "y", s))
        pieces.append(shift(from_y, "x", s))
    parts = attend(place, queries, pieces, state, 1536, True)
    parts = lax.all_to_all(parts, ("zh", "head"), 0, 0, tiled=True)
    return finish(parts, mine, w_out)


def solution(mesh):
    wide = Mesh(mesh.devices.reshape(4, 4, 4, 4), ("y", "zh", "x", "head"))
    seq = ("y", "zh", "x")
    return jax.shard_map(
        body,
        mesh=wide,
        in_specs=(
            P(seq, None),
            P(None, "head"),
            P(None, "head"),
            P(None, "head"),
            P(),
            P(seq),
            P(),
            P(seq),
        ),
        out_specs=P(seq + ("head",), None),
        check_vma=False,
    )
```

```python
import math

import jax
import jax.numpy as jnp
from jax import lax
from jax.experimental import pallas as pl
from jax.experimental.pallas import tpu as pltpu
from jax.sharding import Mesh, PartitionSpec as P

HD = 128
TOK = 512
QUARTER = 128
ROWS = 144
FLAG = 2.0 ** 100
LOW = -1e30
NT = (((1,), (1,)), ((), ()))
MIB = 2 ** 20


def eye():
    return lax.broadcasted_iota(jnp.int32, (128, 128), 0) == lax.broadcasted_iota(jnp.int32, (128, 128), 1)


def to_column(row):
    return jnp.sum(jnp.where(eye(), jnp.broadcast_to(row, (128, 128)), 0.0), axis=1, keepdims=True)


def to_row(column):
    return jnp.sum(jnp.where(eye(), jnp.broadcast_to(column, (128, 128)), 0.0), axis=0, keepdims=True)


def keys_values_kernel(hid, wk, wv, valid, kv_ref, acc):
    step = pl.program_id(0)
    w = jnp.concatenate([wk[...], wv[...]], axis=1)
    part = jnp.dot(hid[...], w, preferred_element_type=jnp.float32)

    @pl.when(step == 0)
    def _():
        acc[...] = part

    @pl.when(step > 0)
    def _():
        acc[...] += part

    @pl.when(step == pl.num_programs(0) - 1)
    def _():
        kv_ref[:, :HD] = acc[:, :HD].astype(jnp.bfloat16)
        for i in range(TOK // 128):
            live = to_column(valid[i:i + 1, :].astype(jnp.float32))
            rows = acc[i * 128:(i + 1) * 128, HD:]
            kv_ref[i * 128:(i + 1) * 128, HD:] = jnp.where(live > 0.5, rows, FLAG).astype(jnp.bfloat16)


def project_keys_values(hidden, wk, wv, valid):
    depth = hidden.shape[1]
    size = depth // 2
    return pl.pallas_call(
        keys_values_kernel,
        grid=(depth // size,),
        in_specs=[
            pl.BlockSpec((TOK, size), lambda k: (0, k)),
            pl.BlockSpec((size, HD), lambda k: (k, 0)),
            pl.BlockSpec((size, HD), lambda k: (k, 0)),
            pl.BlockSpec((4, 128), lambda k: (0, 0)),
        ],
        out_specs=pl.BlockSpec((TOK, 2 * HD), lambda k: (0, 0)),
        out_shape=jax.ShapeDtypeStruct((TOK, 2 * HD), jnp.bfloat16),
        scratch_shapes=[pltpu.VMEM((TOK, 2 * HD), jnp.float32)],
        compiler_params=pltpu.CompilerParams(vmem_limit_bytes=56 * MIB),
        cost_estimate=pl.CostEstimate(flops=4 * TOK * depth * HD, bytes_accessed=8_000_000, transcendentals=0),
        name="keys_values",
    )(hidden, wk, wv, valid.reshape(4, 128))


def queries_kernel(hid, wq, q_ref, acc):
    step = pl.program_id(0)
    part = jnp.dot(hid[...], wq[...], preferred_element_type=jnp.float32)

    @pl.when(step == 0)
    def _():
        acc[...] = part

    @pl.when(step > 0)
    def _():
        acc[...] += part

    @pl.when(step == pl.num_programs(0) - 1)
    def _():
        q_ref[...] = (acc[...] * (math.log2(math.e) / math.sqrt(HD))).astype(jnp.bfloat16)


def project_queries(hidden, wq):
    depth = hidden.shape[1]
    size = depth // 2
    return pl.pallas_call(
        queries_kernel,
        grid=(depth // size,),
        in_specs=[
            pl.BlockSpec((TOK, size), lambda k: (0, k)),
            pl.BlockSpec((size, HD), lambda k: (k, 0)),
        ],
        out_specs=pl.BlockSpec((TOK, HD), lambda k: (0, 0)),
        out_shape=jax.ShapeDtypeStruct((TOK, HD), jnp.bfloat16),
        scratch_shapes=[pltpu.VMEM((TOK, HD), jnp.float32)],
        compiler_params=pltpu.CompilerParams(vmem_limit_bytes=16 * MIB),
        cost_estimate=pl.CostEstimate(flops=2 * TOK * depth * HD, bytes_accessed=6_500_000, transcendentals=0),
        name="queries",
    )(hidden, wq)


def attend_kernel(n_pair, n_kv, chunks, first, last, *refs):
    q_refs = refs[:n_pair]
    kv_refs = refs[n_pair:n_pair + n_kv]
    rest = refs[n_pair + n_kv:]
    n_state = 0 if first else n_pair
    states, rest = rest[:n_state], rest[n_state:]
    outs, (kx, vx) = rest[:-2], rest[-2:]
    start = 0
    for ref in kv_refs:
        size = ref.shape[0]
        lane = lax.broadcasted_iota(jnp.int32, (size, HD), 1)
        vals = ref[:, HD:].astype(jnp.float32)
        live = vals[:, :1] < FLAG * 0.5
        kx[start:start + size, :HD] = ref[:, :HD]
        kx[start:start + size, HD:] = jnp.where((~live) & (lane == 0), LOW, 0.0).astype(jnp.bfloat16)
        vx[start:start + size, :HD] = jnp.where(live, vals, 0.0).astype(jnp.bfloat16)
        vx[start:start + size, HD:] = jnp.where(live & (lane == 0), 1.0, 0.0).astype(jnp.bfloat16)
        start += size
    lane = lax.broadcasted_iota(jnp.int32, (TOK, HD), 1)
    one = jnp.where(lane == 0, 1.0, 0.0).astype(jnp.bfloat16)
    wide = lax.broadcasted_iota(jnp.int32, (TOK, 2 * HD), 1)
    starts = [sum(chunks[:j]) for j in range(len(chunks))]

    for pair in range(n_pair):
        def block(i):
            q = jnp.concatenate([q_refs[pair][i * TOK:(i + 1) * TOK, :], one], axis=1)

            def score(j):
                return lax.dot_general(
                    q, kx[starts[j]:starts[j] + chunks[j], :], NT, preferred_element_type=jnp.float32)

            if first:
                peak = jnp.full((TOK, 1), LOW, jnp.float32)
                acc = jnp.zeros((TOK, 2 * HD), jnp.float32)
            else:
                acc = states[pair][i]
                peak = acc[:, HD + 1:HD + 2]
            s = score(0)
            for j in range(len(chunks)):
                ahead = score(j + 1) if j + 1 < len(chunks) else None
                new_peak = jnp.maximum(peak, jnp.max(s, axis=1, keepdims=True))
                factor = jnp.exp2(peak - new_peak)
                weights = jnp.exp2(s - new_peak).astype(jnp.bfloat16)
                acc = acc * factor + jnp.dot(
                    weights, vx[starts[j]:starts[j] + chunks[j], :], preferred_element_type=jnp.float32)
                peak = new_peak
                s = ahead
            if not last:
                outs[0][pair * 2 + i] = jnp.where(wide == HD + 1, peak, acc)
            else:
                mass = acc[:, HD:HD + 1]
                result = (acc[:, :HD] / mass).astype(jnp.bfloat16)
                logs = peak + jnp.log2(mass)
                out = outs[pair * 2 + i]
                for k in range(4):
                    out[k, :QUARTER, :] = result[k * QUARTER:(k + 1) * QUARTER, :]
                    row = to_row(logs[k * QUARTER:(k + 1) * QUARTER, :])
                    high = row.astype(jnp.bfloat16).astype(jnp.float32)
                    mid = (row - high).astype(jnp.bfloat16).astype(jnp.float32)
                    low = row - high - mid
                    sub = lax.broadcasted_iota(jnp.int32, (ROWS - QUARTER, 128), 0)
                    tile = jnp.where(sub == 0, high, jnp.where(sub == 1, mid, jnp.where(sub == 2, low, 0.0)))
                    out[k, QUARTER:, :] = tile.astype(jnp.bfloat16)

        for i in range(2):
            block(i)


def attend(pairs, pieces, states, chunks, last):
    total = sum(p.shape[0] for p in pieces)
    assert sum(chunks) == total
    n = len(pairs)
    first = states is None
    if last:
        out = [jax.ShapeDtypeStruct((4, ROWS, HD), jnp.bfloat16)] * (2 * n)
    else:
        out = [jax.ShapeDtypeStruct((2 * n, TOK, 2 * HD), jnp.float32)]
    args = list(pairs) + list(pieces) + ([] if first else list(states))

    def kernel(*refs):
        attend_kernel(n, len(pieces), chunks, first, last, *refs)

    return pl.pallas_call(
        kernel,
        in_specs=[pl.BlockSpec(memory_space=pltpu.VMEM)] * len(args),
        out_specs=[pl.BlockSpec(memory_space=pltpu.VMEM)] * len(out),
        out_shape=out,
        scratch_shapes=[
            pltpu.VMEM((total, 2 * HD), jnp.bfloat16),
            pltpu.VMEM((total, 2 * HD), jnp.bfloat16),
        ],
        compiler_params=pltpu.CompilerParams(vmem_limit_bytes=30 * MIB),
        cost_estimate=pl.CostEstimate(
            flops=16 * n * TOK * total * HD, bytes_accessed=total * 512 + n * TOK * 2048,
            transcendentals=2 * n * TOK * total),
        name="attend",
    )(*args)


def combine_kernel(p0, p1, p2, p3, chosen, out):
    parts = (p0, p1, p2, p3)
    for k in range(4):
        logs = []
        for part in parts:
            tile = part[k, QUARTER:, :].astype(jnp.float32)
            logs.append(tile[0:1, :] + tile[1:2, :] + tile[2:3, :])
        top = jnp.maximum(jnp.maximum(logs[0], logs[1]), jnp.maximum(logs[2], logs[3]))
        shares = [jnp.exp2(x - top) for x in logs]
        whole = shares[0] + shares[1] + shares[2] + shares[3]
        acc = jnp.zeros((QUARTER, HD), jnp.float32)
        for share, part in zip(shares, parts):
            acc += to_column(share / whole) * part[k, :QUARTER, :].astype(jnp.float32)
        picked = to_column(chosen[k:k + 1, :].astype(jnp.float32)) > 0.5
        out[k] = jnp.where(picked, acc, 0.0).astype(jnp.bfloat16)


def combine(parts, chosen):
    return pl.pallas_call(
        combine_kernel,
        in_specs=[pl.BlockSpec(memory_space=pltpu.VMEM)] * 5,
        out_specs=pl.BlockSpec(memory_space=pltpu.VMEM),
        out_shape=jax.ShapeDtypeStruct((4, QUARTER, HD), jnp.bfloat16),
        compiler_params=pltpu.CompilerParams(vmem_limit_bytes=16 * MIB),
        cost_estimate=pl.CostEstimate(flops=4_000_000, bytes_accessed=800_000, transcendentals=8192),
        name="combine",
    )(*parts, chosen)


def finish_kernel(heads, w, out, mixed):
    @pl.when(pl.program_id(0) == 0)
    def _():
        for h in range(4):
            mixed[:, h * HD:(h + 1) * HD] = heads[h]

    out[...] = jnp.dot(mixed[...], w[...], preferred_element_type=jnp.float32).astype(jnp.bfloat16)


def finish(heads, w_out):
    width = w_out.shape[1]
    size = 2560
    return pl.pallas_call(
        finish_kernel,
        grid=(width // size,),
        in_specs=[
            pl.BlockSpec((4, QUARTER, HD), lambda j: (0, 0, 0)),
            pl.BlockSpec((4 * HD, size), lambda j: (0, j)),
        ],
        out_specs=pl.BlockSpec((QUARTER, size), lambda j: (0, j)),
        out_shape=jax.ShapeDtypeStruct((QUARTER, width), jnp.bfloat16),
        scratch_shapes=[pltpu.VMEM((QUARTER, 4 * HD), jnp.bfloat16)],
        compiler_params=pltpu.CompilerParams(vmem_limit_bytes=16 * MIB),
        cost_estimate=pl.CostEstimate(flops=2 * QUARTER * 4 * HD * width, bytes_accessed=7_000_000, transcendentals=0),
        name="finish",
    )(heads, w_out)


def shift(x, axis, by):
    return lax.ppermute(x, axis, [(i, (i + by) % 4) for i in range(4)])


def swap(x, axis, by):
    return lax.ppermute(x, axis, [(i, i ^ by) for i in range(4)])


def body(hidden, w_query, w_key, w_value, w_out, valid, window, frame_ids):
    chosen = jnp.any(frame_ids[:, None] == window[None, :], axis=1) & (valid > 0)
    chosen = chosen.astype(jnp.int32).reshape(4, QUARTER)
    h = TOK // 2
    kv = project_keys_values(hidden, w_key, w_value, valid)
    x1, x3, y1, y3 = shift(kv, "x", 1), shift(kv, "x", 3), shift(kv, "y", 1), shift(kv, "y", 3)
    late, _ = lax.optimization_barrier((hidden, kv))
    q = project_queries(late, w_query)
    near = jnp.concatenate([q, swap(q, "zh", 1)], axis=0)
    v1 = shift(jnp.concatenate([x1[:h], x3[:h], y1[:h]], axis=0), "y", 1)
    v3 = shift(jnp.concatenate([x1[:h], x3[:h], y3[h:]], axis=0), "y", 3)
    u1 = shift(jnp.concatenate([y1[h:], y3[h:], x1[:h]], axis=0), "x", 1)
    u3 = shift(jnp.concatenate([y1[h:], y3[h:], x3[h:]], axis=0), "x", 3)
    far = swap(near, "zh", 2)
    (state,) = attend([near], [kv, x1, x3, y1, y3], None, (1280, 1280), False)
    opposite = [(i * 4 + j, ((i + 2) % 4) * 4 + (j + 2) % 4) for i in range(4) for j in range(4)]
    corner = lax.ppermute(kv, ("y", "x"), opposite)
    s1 = shift(jnp.concatenate([v1[:h], v3[:h]], axis=0), "x", 1)
    s3 = shift(u3[:2 * h], "x", 3)
    t1 = shift(jnp.concatenate([u1[:h], u3[:h]], axis=0), "y", 1)
    t3 = shift(v3[:2 * h], "y", 3)
    (state_far,) = attend(
        [far], [kv, x1, x3, y1, y3, u1, u3, v1, v3], None, (1280, 1280, 1536, 1536), False)
    (state,) = attend([near], [u1, u3, v1, v3], [state], (1536, 1536), False)
    rest = [s1, s3, t1, t3, corner]
    o2, o3 = attend([far], rest, [state_far], (1280, 1280), True)
    o2, o3 = swap(o2, "zh", 2), swap(o3, "zh", 3)
    o0, o1 = attend([near], rest, [state], (1280, 1280), True)
    o1 = swap(o1, "zh", 1)
    attended = combine([o0, o1, o2, o3], chosen)
    heads = lax.all_to_all(attended, "head", 0, 0, tiled=True)
    return finish(heads, w_out)


def solution(mesh):
    wide = Mesh(mesh.devices.reshape(4, 4, 4, 4), ("y", "zh", "x", "head"))
    seq = ("y", "zh", "x")
    return jax.shard_map(
        body,
        mesh=wide,
        in_specs=(
            P(seq, None),
            P(None, "head"),
            P(None, "head"),
            P(None, "head"),
            P(),
            P(seq),
            P(),
            P(seq),
        ),
        out_specs=P(seq + ("head",), None),
        check_vma=False,
    )
```

```python
import math

import jax
import jax.numpy as jnp
from jax import lax
from jax.experimental import pallas as pl
from jax.experimental.pallas import tpu as pltpu
from jax.sharding import Mesh, PartitionSpec as P

HD = 128
TOK = 512
QUARTER = 128
ROWS = 144
FLAG = 2.0 ** 100
LOW = -1e30
NT = (((1,), (1,)), ((), ()))
MIB = 2 ** 20


def eye():
    return lax.broadcasted_iota(jnp.int32, (128, 128), 0) == lax.broadcasted_iota(jnp.int32, (128, 128), 1)


def to_column(row):
    return jnp.sum(jnp.where(eye(), jnp.broadcast_to(row, (128, 128)), 0.0), axis=1, keepdims=True)


def to_row(column):
    return jnp.sum(jnp.where(eye(), jnp.broadcast_to(column, (128, 128)), 0.0), axis=0, keepdims=True)


def keys_values_kernel(hid, wk, wv, valid, kv_ref, acc):
    step = pl.program_id(0)
    w = jnp.concatenate([wk[...], wv[...]], axis=1)
    part = jnp.dot(hid[...], w, preferred_element_type=jnp.float32)

    @pl.when(step == 0)
    def _():
        acc[...] = part

    @pl.when(step > 0)
    def _():
        acc[...] += part

    @pl.when(step == pl.num_programs(0) - 1)
    def _():
        kv_ref[:, :HD] = acc[:, :HD].astype(jnp.bfloat16)
        for i in range(TOK // 128):
            live = to_column(valid[i:i + 1, :].astype(jnp.float32))
            rows = acc[i * 128:(i + 1) * 128, HD:]
            kv_ref[i * 128:(i + 1) * 128, HD:] = jnp.where(live > 0.5, rows, FLAG).astype(jnp.bfloat16)


def project_keys_values(hidden, wk, wv, valid):
    depth = hidden.shape[1]
    size = depth // 2
    return pl.pallas_call(
        keys_values_kernel,
        grid=(depth // size,),
        in_specs=[
            pl.BlockSpec((TOK, size), lambda k: (0, k)),
            pl.BlockSpec((size, HD), lambda k: (k, 0)),
            pl.BlockSpec((size, HD), lambda k: (k, 0)),
            pl.BlockSpec((4, 128), lambda k: (0, 0)),
        ],
        out_specs=pl.BlockSpec((TOK, 2 * HD), lambda k: (0, 0)),
        out_shape=jax.ShapeDtypeStruct((TOK, 2 * HD), jnp.bfloat16),
        scratch_shapes=[pltpu.VMEM((TOK, 2 * HD), jnp.float32)],
        compiler_params=pltpu.CompilerParams(vmem_limit_bytes=56 * MIB),
        cost_estimate=pl.CostEstimate(flops=4 * TOK * depth * HD, bytes_accessed=8_000_000, transcendentals=0),
        name="keys_values",
    )(hidden, wk, wv, valid.reshape(4, 128))


def queries_kernel(hid, wq, q_ref, acc):
    step = pl.program_id(0)
    part = jnp.dot(hid[...], wq[...], preferred_element_type=jnp.float32)

    @pl.when(step == 0)
    def _():
        acc[...] = part

    @pl.when(step > 0)
    def _():
        acc[...] += part

    @pl.when(step == pl.num_programs(0) - 1)
    def _():
        q_ref[...] = (acc[...] * (math.log2(math.e) / math.sqrt(HD))).astype(jnp.bfloat16)


def project_queries(hidden, wq):
    depth = hidden.shape[1]
    size = depth // 2
    return pl.pallas_call(
        queries_kernel,
        grid=(depth // size,),
        in_specs=[
            pl.BlockSpec((TOK, size), lambda k: (0, k)),
            pl.BlockSpec((size, HD), lambda k: (k, 0)),
        ],
        out_specs=pl.BlockSpec((TOK, HD), lambda k: (0, 0)),
        out_shape=jax.ShapeDtypeStruct((TOK, HD), jnp.bfloat16),
        scratch_shapes=[pltpu.VMEM((TOK, HD), jnp.float32)],
        compiler_params=pltpu.CompilerParams(vmem_limit_bytes=16 * MIB),
        cost_estimate=pl.CostEstimate(flops=2 * TOK * depth * HD, bytes_accessed=6_500_000, transcendentals=0),
        name="queries",
    )(hidden, wq)


def attend_kernel(n_pair, n_kv, chunks, first, last, *refs):
    q_refs = refs[:n_pair]
    kv_refs = refs[n_pair:n_pair + n_kv]
    rest = refs[n_pair + n_kv:]
    n_state = 0 if first else n_pair
    states, rest = rest[:n_state], rest[n_state:]
    outs, (kx, vx) = rest[:-2], rest[-2:]
    start = 0
    for ref in kv_refs:
        size = ref.shape[0]
        lane = lax.broadcasted_iota(jnp.int32, (size, HD), 1)
        vals = ref[:, HD:].astype(jnp.float32)
        live = vals[:, :1] < FLAG * 0.5
        kx[start:start + size, :HD] = ref[:, :HD]
        kx[start:start + size, HD:] = jnp.where((~live) & (lane == 0), LOW, 0.0).astype(jnp.bfloat16)
        vx[start:start + size, :HD] = jnp.where(live, vals, 0.0).astype(jnp.bfloat16)
        vx[start:start + size, HD:] = jnp.where(live & (lane == 0), 1.0, 0.0).astype(jnp.bfloat16)
        start += size
    lane = lax.broadcasted_iota(jnp.int32, (TOK, HD), 1)
    one = jnp.where(lane == 0, 1.0, 0.0).astype(jnp.bfloat16)
    wide = lax.broadcasted_iota(jnp.int32, (TOK, 2 * HD), 1)
    starts = [sum(chunks[:j]) for j in range(len(chunks))]

    for pair in range(n_pair):
        def block(i):
            q = jnp.concatenate([q_refs[pair][i * TOK:(i + 1) * TOK, :], one], axis=1)

            def score(j):
                return lax.dot_general(
                    q, kx[starts[j]:starts[j] + chunks[j], :], NT, preferred_element_type=jnp.float32)

            if first:
                peak = jnp.full((TOK, 1), LOW, jnp.float32)
                acc = jnp.zeros((TOK, 2 * HD), jnp.float32)
            else:
                acc = states[pair][i]
                peak = acc[:, HD + 1:HD + 2]
            s = score(0)
            for j in range(len(chunks)):
                ahead = score(j + 1) if j + 1 < len(chunks) else None
                new_peak = jnp.maximum(peak, jnp.max(s, axis=1, keepdims=True))
                factor = jnp.exp2(peak - new_peak)
                weights = jnp.exp2(s - new_peak).astype(jnp.bfloat16)
                acc = acc * factor + jnp.dot(
                    weights, vx[starts[j]:starts[j] + chunks[j], :], preferred_element_type=jnp.float32)
                peak = new_peak
                s = ahead
            if not last:
                outs[0][pair * 2 + i] = jnp.where(wide == HD + 1, peak, acc)
            else:
                mass = acc[:, HD:HD + 1]
                result = (acc[:, :HD] / mass).astype(jnp.bfloat16)
                logs = peak + jnp.log2(mass)
                out = outs[pair * 2 + i]
                for k in range(4):
                    out[k, :QUARTER, :] = result[k * QUARTER:(k + 1) * QUARTER, :]
                    row = to_row(logs[k * QUARTER:(k + 1) * QUARTER, :])
                    high = row.astype(jnp.bfloat16).astype(jnp.float32)
                    mid = (row - high).astype(jnp.bfloat16).astype(jnp.float32)
                    low = row - high - mid
                    sub = lax.broadcasted_iota(jnp.int32, (ROWS - QUARTER, 128), 0)
                    tile = jnp.where(sub == 0, high, jnp.where(sub == 1, mid, jnp.where(sub == 2, low, 0.0)))
                    out[k, QUARTER:, :] = tile.astype(jnp.bfloat16)

        for i in range(2):
            block(i)


def attend(pairs, pieces, states, chunks, last):
    total = sum(p.shape[0] for p in pieces)
    assert sum(chunks) == total
    n = len(pairs)
    first = states is None
    if last:
        out = [jax.ShapeDtypeStruct((4, ROWS, HD), jnp.bfloat16)] * (2 * n)
    else:
        out = [jax.ShapeDtypeStruct((2 * n, TOK, 2 * HD), jnp.float32)]
    args = list(pairs) + list(pieces) + ([] if first else list(states))

    def kernel(*refs):
        attend_kernel(n, len(pieces), chunks, first, last, *refs)

    return pl.pallas_call(
        kernel,
        in_specs=[pl.BlockSpec(memory_space=pltpu.VMEM)] * len(args),
        out_specs=[pl.BlockSpec(memory_space=pltpu.VMEM)] * len(out),
        out_shape=out,
        scratch_shapes=[
            pltpu.VMEM((total, 2 * HD), jnp.bfloat16),
            pltpu.VMEM((total, 2 * HD), jnp.bfloat16),
        ],
        compiler_params=pltpu.CompilerParams(vmem_limit_bytes=30 * MIB),
        cost_estimate=pl.CostEstimate(
            flops=16 * n * TOK * total * HD, bytes_accessed=total * 512 + n * TOK * 2048,
            transcendentals=2 * n * TOK * total),
        name="attend",
    )(*args)


def combine_kernel(p0, p1, p2, p3, chosen, place, keep, give):
    parts = (p0, p1, p2, p3)
    core = lax.rem(place[0], 2)
    for k in range(4):
        logs = []
        for part in parts:
            tile = part[k, QUARTER:, :].astype(jnp.float32)
            logs.append(tile[0:1, :] + tile[1:2, :] + tile[2:3, :])
        top = jnp.maximum(jnp.maximum(logs[0], logs[1]), jnp.maximum(logs[2], logs[3]))
        shares = [jnp.exp2(x - top) for x in logs]
        whole = shares[0] + shares[1] + shares[2] + shares[3]
        acc = jnp.zeros((QUARTER, HD), jnp.float32)
        for share, part in zip(shares, parts):
            acc += to_column(share / whole) * part[k, :QUARTER, :].astype(jnp.float32)
        picked = to_column(chosen[k:k + 1, :].astype(jnp.float32)) > 0.5
        value = jnp.where(picked, acc, 0.0).astype(jnp.bfloat16)

        @pl.when(core == k % 2)
        def _():
            keep[k // 2] = value

        @pl.when(core != k % 2)
        def _():
            give[k // 2] = value


def combine(parts, chosen, place):
    half = jax.ShapeDtypeStruct((2, QUARTER, HD), jnp.bfloat16)
    return pl.pallas_call(
        combine_kernel,
        in_specs=[pl.BlockSpec(memory_space=pltpu.VMEM)] * 5 + [pl.BlockSpec(memory_space=pltpu.SMEM)],
        out_specs=[pl.BlockSpec(memory_space=pltpu.VMEM)] * 2,
        out_shape=[half, half],
        compiler_params=pltpu.CompilerParams(vmem_limit_bytes=16 * MIB),
        cost_estimate=pl.CostEstimate(flops=4_000_000, bytes_accessed=800_000, transcendentals=8192),
        name="combine",
    )(*parts, chosen, place)


def choose_kernel(keep, got, place, mine, theirs):
    high = lax.div(place[0], 2)
    mine[0] = keep[high]
    mine[1] = got[high]
    theirs[0] = keep[1 - high]
    theirs[1] = got[1 - high]


def choose(keep, got, place):
    half = jax.ShapeDtypeStruct((2, QUARTER, HD), jnp.bfloat16)
    return pl.pallas_call(
        choose_kernel,
        in_specs=[pl.BlockSpec(memory_space=pltpu.VMEM)] * 2 + [pl.BlockSpec(memory_space=pltpu.SMEM)],
        out_specs=[pl.BlockSpec(memory_space=pltpu.VMEM)] * 2,
        out_shape=[half, half],
        compiler_params=pltpu.CompilerParams(vmem_limit_bytes=16 * MIB),
        cost_estimate=pl.CostEstimate(flops=0, bytes_accessed=300_000, transcendentals=0),
        name="choose",
    )(keep, got, place)


def finish_kernel(mine, theirs, place, w, out, mixed):
    @pl.when(pl.program_id(0) == 0)
    def _():
        for slot, ref in ((0, mine), (2, theirs)):
            for j in range(2):
                head = lax.bitwise_xor(place[0], slot + j)
                mixed[:, pl.ds(pl.multiple_of(head * HD, HD), HD)] = ref[j]

    out[...] = jnp.dot(mixed[...], w[...], preferred_element_type=jnp.float32).astype(jnp.bfloat16)


def finish(mine, theirs, w_out, place):
    width = w_out.shape[1]
    size = 2560
    return pl.pallas_call(
        finish_kernel,
        grid=(width // size,),
        in_specs=[
            pl.BlockSpec((2, QUARTER, HD), lambda j: (0, 0, 0)),
            pl.BlockSpec((2, QUARTER, HD), lambda j: (0, 0, 0)),
            pl.BlockSpec(memory_space=pltpu.SMEM),
            pl.BlockSpec((4 * HD, size), lambda j: (0, j)),
        ],
        out_specs=pl.BlockSpec((QUARTER, size), lambda j: (0, j)),
        out_shape=jax.ShapeDtypeStruct((QUARTER, width), jnp.bfloat16),
        scratch_shapes=[pltpu.VMEM((QUARTER, 4 * HD), jnp.bfloat16)],
        compiler_params=pltpu.CompilerParams(vmem_limit_bytes=16 * MIB),
        cost_estimate=pl.CostEstimate(flops=2 * QUARTER * 4 * HD * width, bytes_accessed=7_000_000, transcendentals=0),
        name="finish",
    )(mine, theirs, place, w_out)


def shift(x, axis, by):
    return lax.ppermute(x, axis, [(i, (i + by) % 4) for i in range(4)])


def swap(x, axis, by):
    return lax.ppermute(x, axis, [(i, i ^ by) for i in range(4)])


def body(hidden, w_query, w_key, w_value, w_out, valid, window, frame_ids):
    chosen = jnp.any(frame_ids[:, None] == window[None, :], axis=1) & (valid > 0)
    chosen = chosen.astype(jnp.int32).reshape(4, QUARTER)
    h = TOK // 2
    kv = project_keys_values(hidden, w_key, w_value, valid)
    x1, x3, y1, y3 = shift(kv, "x", 1), shift(kv, "x", 3), shift(kv, "y", 1), shift(kv, "y", 3)
    late, _ = lax.optimization_barrier((hidden, kv))
    q = project_queries(late, w_query)
    near = jnp.concatenate([q, swap(q, "zh", 1)], axis=0)
    v1 = shift(jnp.concatenate([x1[:h], x3[:h], y1[:h]], axis=0), "y", 1)
    v3 = shift(jnp.concatenate([x1[:h], x3[:h], y3[h:]], axis=0), "y", 3)
    u1 = shift(jnp.concatenate([y1[h:], y3[h:], x1[:h]], axis=0), "x", 1)
    u3 = shift(jnp.concatenate([y1[h:], y3[h:], x3[h:]], axis=0), "x", 3)
    far = swap(near, "zh", 2)
    (state,) = attend([near], [kv, x1, x3, y1, y3], None, (1280, 1280), False)
    opposite = [(i * 4 + j, ((i + 2) % 4) * 4 + (j + 2) % 4) for i in range(4) for j in range(4)]
    corner = lax.ppermute(kv, ("y", "x"), opposite)
    s1 = shift(jnp.concatenate([v1[:h], v3[:h]], axis=0), "x", 1)
    s3 = shift(u3[:2 * h], "x", 3)
    t1 = shift(jnp.concatenate([u1[:h], u3[:h]], axis=0), "y", 1)
    t3 = shift(v3[:2 * h], "y", 3)
    (state_far,) = attend(
        [far], [kv, x1, x3, y1, y3, u1, u3, v1, v3], None, (1280, 1280, 1536, 1536), False)
    (state,) = attend([near], [u1, u3, v1, v3], [state], (1536, 1536), False)
    rest = [s1, s3, t1, t3, corner]
    o2, o3 = attend([far], rest, [state_far], (1280, 1280), True)
    o2, o3 = swap(o2, "zh", 2), swap(o3, "zh", 3)
    o0, o1 = attend([near], rest, [state], (1280, 1280), True)
    o1 = swap(o1, "zh", 1)
    place = lax.axis_index("head").astype(jnp.int32).reshape(1)
    keep, give = combine([o0, o1, o2, o3], chosen, place)
    got = swap(give, "head", 1)
    mine, theirs = choose(keep, got, place)
    return finish(mine, swap(theirs, "head", 2), w_out, place)


def solution(mesh):
    wide = Mesh(mesh.devices.reshape(4, 4, 4, 4), ("y", "zh", "x", "head"))
    seq = ("y", "zh", "x")
    return jax.shard_map(
        body,
        mesh=wide,
        in_specs=(
            P(seq, None),
            P(None, "head"),
            P(None, "head"),
            P(None, "head"),
            P(),
            P(seq),
            P(),
            P(seq),
        ),
        out_specs=P(seq + ("head",), None),
        check_vma=False,
    )
```

```python
import math

import jax
import jax.numpy as jnp
from jax import lax
from jax.experimental import pallas as pl
from jax.experimental.pallas import tpu as pltpu
from jax.sharding import Mesh, PartitionSpec as P

HD = 128
TOK = 512
QUARTER = 128
ROWS = 144
FLAG = 2.0 ** 100
LOW = -1e30
NT = (((1,), (1,)), ((), ()))
MIB = 2 ** 20


def eye():
    return lax.broadcasted_iota(jnp.int32, (128, 128), 0) == lax.broadcasted_iota(jnp.int32, (128, 128), 1)


def to_column(row):
    return jnp.sum(jnp.where(eye(), jnp.broadcast_to(row, (128, 128)), 0.0), axis=1, keepdims=True)


def to_row(column):
    return jnp.sum(jnp.where(eye(), jnp.broadcast_to(column, (128, 128)), 0.0), axis=0, keepdims=True)


def keys_values_kernel(hid, wk, wv, valid, kv_ref, acc):
    step = pl.program_id(0)
    w = jnp.concatenate([wk[...], wv[...]], axis=1)
    part = jnp.dot(hid[...], w, preferred_element_type=jnp.float32)

    @pl.when(step == 0)
    def _():
        acc[...] = part

    @pl.when(step > 0)
    def _():
        acc[...] += part

    @pl.when(step == pl.num_programs(0) - 1)
    def _():
        kv_ref[:, :HD] = acc[:, :HD].astype(jnp.bfloat16)
        for i in range(TOK // 128):
            live = to_column(valid[i:i + 1, :].astype(jnp.float32))
            rows = acc[i * 128:(i + 1) * 128, HD:]
            kv_ref[i * 128:(i + 1) * 128, HD:] = jnp.where(live > 0.5, rows, FLAG).astype(jnp.bfloat16)


def project_keys_values(hidden, wk, wv, valid):
    depth = hidden.shape[1]
    size = depth // 2
    return pl.pallas_call(
        keys_values_kernel,
        grid=(depth // size,),
        in_specs=[
            pl.BlockSpec((TOK, size), lambda k: (0, k)),
            pl.BlockSpec((size, HD), lambda k: (k, 0)),
            pl.BlockSpec((size, HD), lambda k: (k, 0)),
            pl.BlockSpec((4, 128), lambda k: (0, 0)),
        ],
        out_specs=pl.BlockSpec((TOK, 2 * HD), lambda k: (0, 0)),
        out_shape=jax.ShapeDtypeStruct((TOK, 2 * HD), jnp.bfloat16),
        scratch_shapes=[pltpu.VMEM((TOK, 2 * HD), jnp.float32)],
        compiler_params=pltpu.CompilerParams(vmem_limit_bytes=56 * MIB),
        cost_estimate=pl.CostEstimate(flops=4 * TOK * depth * HD, bytes_accessed=8_000_000, transcendentals=0),
        name="keys_values",
    )(hidden, wk, wv, valid.reshape(4, 128))


def queries_kernel(hid, wq, q_ref, acc):
    step = pl.program_id(0)
    part = jnp.dot(hid[...], wq[...], preferred_element_type=jnp.float32)

    @pl.when(step == 0)
    def _():
        acc[...] = part

    @pl.when(step > 0)
    def _():
        acc[...] += part

    @pl.when(step == pl.num_programs(0) - 1)
    def _():
        q_ref[...] = (acc[...] * (math.log2(math.e) / math.sqrt(HD))).astype(jnp.bfloat16)


def project_queries(hidden, wq):
    depth = hidden.shape[1]
    size = depth // 2
    return pl.pallas_call(
        queries_kernel,
        grid=(depth // size,),
        in_specs=[
            pl.BlockSpec((TOK, size), lambda k: (0, k)),
            pl.BlockSpec((size, HD), lambda k: (k, 0)),
        ],
        out_specs=pl.BlockSpec((TOK, HD), lambda k: (0, 0)),
        out_shape=jax.ShapeDtypeStruct((TOK, HD), jnp.bfloat16),
        scratch_shapes=[pltpu.VMEM((TOK, HD), jnp.float32)],
        compiler_params=pltpu.CompilerParams(vmem_limit_bytes=16 * MIB),
        cost_estimate=pl.CostEstimate(flops=2 * TOK * depth * HD, bytes_accessed=6_500_000, transcendentals=0),
        name="queries",
    )(hidden, wq)


def attend_kernel(n_pair, n_kv, chunks, first, last, *refs):
    q_refs = refs[:n_pair]
    kv_refs = refs[n_pair:n_pair + n_kv]
    rest = refs[n_pair + n_kv:]
    n_state = 0 if first else n_pair
    states, rest = rest[:n_state], rest[n_state:]
    outs, (kx, vx) = rest[:-2], rest[-2:]
    start = 0
    for ref in kv_refs:
        size = ref.shape[0]
        lane = lax.broadcasted_iota(jnp.int32, (size, HD), 1)
        vals = ref[:, HD:].astype(jnp.float32)
        live = vals[:, :1] < FLAG * 0.5
        kx[start:start + size, :HD] = ref[:, :HD]
        kx[start:start + size, HD:] = jnp.where((~live) & (lane == 0), LOW, 0.0).astype(jnp.bfloat16)
        vx[start:start + size, :HD] = jnp.where(live, vals, 0.0).astype(jnp.bfloat16)
        vx[start:start + size, HD:] = jnp.where(live & (lane == 0), 1.0, 0.0).astype(jnp.bfloat16)
        start += size
    lane = lax.broadcasted_iota(jnp.int32, (TOK, HD), 1)
    one = jnp.where(lane == 0, 1.0, 0.0).astype(jnp.bfloat16)
    wide = lax.broadcasted_iota(jnp.int32, (TOK, 2 * HD), 1)
    starts = [sum(chunks[:j]) for j in range(len(chunks))]

    for pair in range(n_pair):
        def block(i):
            q = jnp.concatenate([q_refs[pair][i * TOK:(i + 1) * TOK, :], one], axis=1)

            def score(j):
                return lax.dot_general(
                    q, kx[starts[j]:starts[j] + chunks[j], :], NT, preferred_element_type=jnp.float32)

            if first:
                peak = jnp.full((TOK, 1), LOW, jnp.float32)
                acc = jnp.zeros((TOK, 2 * HD), jnp.float32)
            else:
                acc = states[pair][i]
                peak = acc[:, HD + 1:HD + 2]
            s = score(0)
            for j in range(len(chunks)):
                ahead = score(j + 1) if j + 1 < len(chunks) else None
                new_peak = jnp.maximum(peak, jnp.max(s, axis=1, keepdims=True))
                factor = jnp.exp2(peak - new_peak)
                weights = jnp.exp2(s - new_peak).astype(jnp.bfloat16)
                acc = acc * factor + jnp.dot(
                    weights, vx[starts[j]:starts[j] + chunks[j], :], preferred_element_type=jnp.float32)
                peak = new_peak
                s = ahead
            if not last:
                outs[0][pair * 2 + i] = jnp.where(wide == HD + 1, peak, acc)
            else:
                mass = acc[:, HD:HD + 1]
                result = (acc[:, :HD] / mass).astype(jnp.bfloat16)
                logs = peak + jnp.log2(mass)
                out = outs[pair * 2 + i]
                for k in range(4):
                    out[k, :QUARTER, :] = result[k * QUARTER:(k + 1) * QUARTER, :]
                    row = to_row(logs[k * QUARTER:(k + 1) * QUARTER, :])
                    high = row.astype(jnp.bfloat16).astype(jnp.float32)
                    mid = (row - high).astype(jnp.bfloat16).astype(jnp.float32)
                    low = row - high - mid
                    sub = lax.broadcasted_iota(jnp.int32, (ROWS - QUARTER, 128), 0)
                    tile = jnp.where(sub == 0, high, jnp.where(sub == 1, mid, jnp.where(sub == 2, low, 0.0)))
                    out[k, QUARTER:, :] = tile.astype(jnp.bfloat16)

        for i in range(2):
            block(i)


def attend(pairs, pieces, states, chunks, last):
    total = sum(p.shape[0] for p in pieces)
    assert sum(chunks) == total
    n = len(pairs)
    first = states is None
    if last:
        out = [jax.ShapeDtypeStruct((4, ROWS, HD), jnp.bfloat16)] * (2 * n)
    else:
        out = [jax.ShapeDtypeStruct((2 * n, TOK, 2 * HD), jnp.float32)]
    args = list(pairs) + list(pieces) + ([] if first else list(states))

    def kernel(*refs):
        attend_kernel(n, len(pieces), chunks, first, last, *refs)

    return pl.pallas_call(
        kernel,
        in_specs=[pl.BlockSpec(memory_space=pltpu.VMEM)] * len(args),
        out_specs=[pl.BlockSpec(memory_space=pltpu.VMEM)] * len(out),
        out_shape=out,
        scratch_shapes=[
            pltpu.VMEM((total, 2 * HD), jnp.bfloat16),
            pltpu.VMEM((total, 2 * HD), jnp.bfloat16),
        ],
        compiler_params=pltpu.CompilerParams(vmem_limit_bytes=30 * MIB),
        cost_estimate=pl.CostEstimate(
            flops=16 * n * TOK * total * HD, bytes_accessed=total * 512 + n * TOK * 2048,
            transcendentals=2 * n * TOK * total),
        name="attend",
    )(*args)


def combine_kernel(p0, p1, p2, p3, chosen, place, keep, give):
    parts = (p0, p1, p2, p3)
    core = lax.rem(place[0], 2)
    for k in range(4):
        logs = []
        for part in parts:
            tile = part[k, QUARTER:, :].astype(jnp.float32)
            logs.append(tile[0:1, :] + tile[1:2, :] + tile[2:3, :])
        top = jnp.maximum(jnp.maximum(logs[0], logs[1]), jnp.maximum(logs[2], logs[3]))
        shares = [jnp.exp2(x - top) for x in logs]
        whole = shares[0] + shares[1] + shares[2] + shares[3]
        acc = jnp.zeros((QUARTER, HD), jnp.float32)
        for share, part in zip(shares, parts):
            acc += to_column(share / whole) * part[k, :QUARTER, :].astype(jnp.float32)
        picked = to_column(chosen[k:k + 1, :].astype(jnp.float32)) > 0.5
        value = jnp.where(picked, acc, 0.0).astype(jnp.bfloat16)

        @pl.when(core == k % 2)
        def _():
            keep[k // 2] = value

        @pl.when(core != k % 2)
        def _():
            give[k // 2] = value


def combine(parts, chosen, place):
    half = jax.ShapeDtypeStruct((2, QUARTER, HD), jnp.bfloat16)
    return pl.pallas_call(
        combine_kernel,
        in_specs=[pl.BlockSpec(memory_space=pltpu.VMEM)] * 5 + [pl.BlockSpec(memory_space=pltpu.SMEM)],
        out_specs=[pl.BlockSpec(memory_space=pltpu.VMEM)] * 2,
        out_shape=[half, half],
        compiler_params=pltpu.CompilerParams(vmem_limit_bytes=16 * MIB),
        cost_estimate=pl.CostEstimate(flops=4_000_000, bytes_accessed=800_000, transcendentals=8192),
        name="combine",
    )(*parts, chosen, place)


def choose_kernel(keep, got, place, mine, theirs):
    high = lax.div(place[0], 2)
    mine[0] = keep[high]
    mine[1] = got[high]
    theirs[0] = keep[1 - high]
    theirs[1] = got[1 - high]


def choose(keep, got, place):
    half = jax.ShapeDtypeStruct((2, QUARTER, HD), jnp.bfloat16)
    return pl.pallas_call(
        choose_kernel,
        in_specs=[pl.BlockSpec(memory_space=pltpu.VMEM)] * 2 + [pl.BlockSpec(memory_space=pltpu.SMEM)],
        out_specs=[pl.BlockSpec(memory_space=pltpu.VMEM)] * 2,
        out_shape=[half, half],
        compiler_params=pltpu.CompilerParams(vmem_limit_bytes=16 * MIB),
        cost_estimate=pl.CostEstimate(flops=0, bytes_accessed=300_000, transcendentals=0),
        name="choose",
    )(keep, got, place)


def finish_kernel(mine, theirs, place, w, out, mixed):
    @pl.when(pl.program_id(0) == 0)
    def _():
        for slot, ref in ((0, mine), (2, theirs)):
            for j in range(2):
                head = lax.bitwise_xor(place[0], slot + j)
                mixed[:, pl.ds(pl.multiple_of(head * HD, HD), HD)] = ref[j]

    out[...] = jnp.dot(mixed[...], w[...], preferred_element_type=jnp.float32).astype(jnp.bfloat16)


def finish(mine, theirs, w_out, place):
    width = w_out.shape[1]
    size = 2560
    return pl.pallas_call(
        finish_kernel,
        grid=(width // size,),
        in_specs=[
            pl.BlockSpec((2, QUARTER, HD), lambda j: (0, 0, 0)),
            pl.BlockSpec((2, QUARTER, HD), lambda j: (0, 0, 0)),
            pl.BlockSpec(memory_space=pltpu.SMEM),
            pl.BlockSpec((4 * HD, size), lambda j: (0, j)),
        ],
        out_specs=pl.BlockSpec((QUARTER, size), lambda j: (0, j)),
        out_shape=jax.ShapeDtypeStruct((QUARTER, width), jnp.bfloat16),
        scratch_shapes=[pltpu.VMEM((QUARTER, 4 * HD), jnp.bfloat16)],
        compiler_params=pltpu.CompilerParams(vmem_limit_bytes=16 * MIB),
        cost_estimate=pl.CostEstimate(flops=2 * QUARTER * 4 * HD * width, bytes_accessed=7_000_000, transcendentals=0),
        name="finish",
    )(mine, theirs, place, w_out)


def shift(x, axis, by):
    return lax.ppermute(x, axis, [(i, (i + by) % 4) for i in range(4)])


def swap(x, axis, by):
    return lax.ppermute(x, axis, [(i, i ^ by) for i in range(4)])


def body(hidden, w_query, w_key, w_value, w_out, valid, window, frame_ids):
    chosen = jnp.any(frame_ids[:, None] == window[None, :], axis=1) & (valid > 0)
    chosen = chosen.astype(jnp.int32).reshape(4, QUARTER)
    h = TOK // 2
    kv = project_keys_values(hidden, w_key, w_value, valid)
    x1, x3, y1, y3 = shift(kv, "x", 1), shift(kv, "x", 3), shift(kv, "y", 1), shift(kv, "y", 3)
    late, _ = lax.optimization_barrier((hidden, kv))
    q = project_queries(late, w_query)
    near = jnp.concatenate([q, swap(q, "zh", 1)], axis=0)
    v1 = shift(jnp.concatenate([x1[:h], x3[:h], y1[:h]], axis=0), "y", 1)
    v3 = shift(jnp.concatenate([x1[:h], x3[:h], y3[h:]], axis=0), "y", 3)
    u1 = shift(jnp.concatenate([y1[h:], y3[h:], x1[:h]], axis=0), "x", 1)
    u3 = shift(jnp.concatenate([y1[h:], y3[h:], x3[h:]], axis=0), "x", 3)
    far = swap(near, "zh", 3)
    (state,) = attend([near], [kv, x1, x3, y1, y3], None, (1280, 1280), False)
    opposite = [(i * 4 + j, ((i + 2) % 4) * 4 + (j + 2) % 4) for i in range(4) for j in range(4)]
    corner = lax.ppermute(kv, ("y", "x"), opposite)
    s1 = shift(jnp.concatenate([v1[:h], v3[:h]], axis=0), "x", 1)
    s3 = shift(u3[:2 * h], "x", 3)
    t1 = shift(jnp.concatenate([u1[:h], u3[:h]], axis=0), "y", 1)
    t3 = shift(v3[:2 * h], "y", 3)
    (state_far,) = attend([far], [kv, x1, x3, y1, y3], None, (1280, 1280), False)
    (state_far,) = attend([far], [u1, u3, v1, v3], [state_far], (1536, 1536), False)
    (state,) = attend([near], [u1, u3, v1, v3], [state], (1536, 1536), False)
    rest = [s1, s3, t1, t3, corner]
    o3, o2 = attend([far], rest, [state_far], (1280, 1280), True)
    o2, o3 = swap(o2, "zh", 2), swap(o3, "zh", 3)
    o0, o1 = attend([near], rest, [state], (1280, 1280), True)
    o1 = swap(o1, "zh", 1)
    place = lax.axis_index("head").astype(jnp.int32).reshape(1)
    keep, give = combine([o0, o1, o2, o3], chosen, place)
    got = swap(give, "head", 1)
    mine, theirs = choose(keep, got, place)
    return finish(mine, swap(theirs, "head", 2), w_out, place)


def solution(mesh):
    wide = Mesh(mesh.devices.reshape(4, 4, 4, 4), ("y", "zh", "x", "head"))
    seq = ("y", "zh", "x")
    return jax.shard_map(
        body,
        mesh=wide,
        in_specs=(
            P(seq, None),
            P(None, "head"),
            P(None, "head"),
            P(None, "head"),
            P(),
            P(seq),
            P(),
            P(seq),
        ),
        out_specs=P(seq + ("head",), None),
        check_vma=False,
    )
```

```python
import math

import jax
import jax.numpy as jnp
from jax import lax
from jax.experimental import pallas as pl
from jax.experimental.pallas import tpu as pltpu
from jax.sharding import Mesh, PartitionSpec as P

HD = 128
TOK = 512
QUARTER = 128
ROWS = 144
FLAG = 2.0 ** 100
LOW = -1e30
NT = (((1,), (1,)), ((), ()))
MIB = 2 ** 20


def eye():
    return lax.broadcasted_iota(jnp.int32, (128, 128), 0) == lax.broadcasted_iota(jnp.int32, (128, 128), 1)


def to_column(row):
    return jnp.sum(jnp.where(eye(), jnp.broadcast_to(row, (128, 128)), 0.0), axis=1, keepdims=True)


def to_row(column):
    return jnp.sum(jnp.where(eye(), jnp.broadcast_to(column, (128, 128)), 0.0), axis=0, keepdims=True)


def keys_values_kernel(hid, wk, wv, valid, kv_ref, acc):
    step = pl.program_id(0)
    w = jnp.concatenate([wk[...], wv[...]], axis=1)
    part = jnp.dot(hid[...], w, preferred_element_type=jnp.float32)

    @pl.when(step == 0)
    def _():
        acc[...] = part

    @pl.when(step > 0)
    def _():
        acc[...] += part

    @pl.when(step == pl.num_programs(0) - 1)
    def _():
        kv_ref[:, :HD] = acc[:, :HD].astype(jnp.bfloat16)
        for i in range(TOK // 128):
            live = to_column(valid[i:i + 1, :].astype(jnp.float32))
            rows = acc[i * 128:(i + 1) * 128, HD:]
            kv_ref[i * 128:(i + 1) * 128, HD:] = jnp.where(live > 0.5, rows, FLAG).astype(jnp.bfloat16)


def project_keys_values(hidden, wk, wv, valid):
    depth = hidden.shape[1]
    size = depth // 2
    return pl.pallas_call(
        keys_values_kernel,
        grid=(depth // size,),
        in_specs=[
            pl.BlockSpec((TOK, size), lambda k: (0, k)),
            pl.BlockSpec((size, HD), lambda k: (k, 0)),
            pl.BlockSpec((size, HD), lambda k: (k, 0)),
            pl.BlockSpec((4, 128), lambda k: (0, 0)),
        ],
        out_specs=pl.BlockSpec((TOK, 2 * HD), lambda k: (0, 0)),
        out_shape=jax.ShapeDtypeStruct((TOK, 2 * HD), jnp.bfloat16),
        scratch_shapes=[pltpu.VMEM((TOK, 2 * HD), jnp.float32)],
        compiler_params=pltpu.CompilerParams(vmem_limit_bytes=56 * MIB),
        cost_estimate=pl.CostEstimate(flops=4 * TOK * depth * HD, bytes_accessed=8_000_000, transcendentals=0),
        name="keys_values",
    )(hidden, wk, wv, valid.reshape(4, 128))


def queries_kernel(hid, wq, q_ref, acc):
    step = pl.program_id(0)
    part = jnp.dot(hid[...], wq[...], preferred_element_type=jnp.float32)

    @pl.when(step == 0)
    def _():
        acc[...] = part

    @pl.when(step > 0)
    def _():
        acc[...] += part

    @pl.when(step == pl.num_programs(0) - 1)
    def _():
        q_ref[...] = (acc[...] * (math.log2(math.e) / math.sqrt(HD))).astype(jnp.bfloat16)


def project_queries(hidden, wq):
    depth = hidden.shape[1]
    size = depth // 2
    return pl.pallas_call(
        queries_kernel,
        grid=(depth // size,),
        in_specs=[
            pl.BlockSpec((TOK, size), lambda k: (0, k)),
            pl.BlockSpec((size, HD), lambda k: (k, 0)),
        ],
        out_specs=pl.BlockSpec((TOK, HD), lambda k: (0, 0)),
        out_shape=jax.ShapeDtypeStruct((TOK, HD), jnp.bfloat16),
        scratch_shapes=[pltpu.VMEM((TOK, HD), jnp.float32)],
        compiler_params=pltpu.CompilerParams(vmem_limit_bytes=16 * MIB),
        cost_estimate=pl.CostEstimate(flops=2 * TOK * depth * HD, bytes_accessed=6_500_000, transcendentals=0),
        name="queries",
    )(hidden, wq)


def attend_kernel(n_pair, n_kv, chunks, first, last, *refs):
    q_refs = refs[:n_pair]
    kv_refs = refs[n_pair:n_pair + n_kv]
    rest = refs[n_pair + n_kv:]
    n_state = 0 if first else n_pair
    states, rest = rest[:n_state], rest[n_state:]
    outs, (kx, vx) = rest[:-2], rest[-2:]
    start = 0
    for ref in kv_refs:
        size = ref.shape[0]
        lane = lax.broadcasted_iota(jnp.int32, (size, HD), 1)
        vals = ref[:, HD:].astype(jnp.float32)
        live = vals[:, :1] < FLAG * 0.5
        kx[start:start + size, :HD] = ref[:, :HD]
        kx[start:start + size, HD:] = jnp.where((~live) & (lane == 0), LOW, 0.0).astype(jnp.bfloat16)
        vx[start:start + size, :HD] = jnp.where(live, vals, 0.0).astype(jnp.bfloat16)
        vx[start:start + size, HD:] = jnp.where(live & (lane == 0), 1.0, 0.0).astype(jnp.bfloat16)
        start += size
    lane = lax.broadcasted_iota(jnp.int32, (TOK, HD), 1)
    one = jnp.where(lane == 0, 1.0, 0.0).astype(jnp.bfloat16)
    wide = lax.broadcasted_iota(jnp.int32, (TOK, 2 * HD), 1)
    starts = [sum(chunks[:j]) for j in range(len(chunks))]

    for pair in range(n_pair):
        def block(i):
            q = jnp.concatenate([q_refs[pair][i * TOK:(i + 1) * TOK, :], one], axis=1)

            def score(j):
                return lax.dot_general(
                    q, kx[starts[j]:starts[j] + chunks[j], :], NT, preferred_element_type=jnp.float32)

            if first:
                peak = jnp.full((TOK, 1), LOW, jnp.float32)
                acc = jnp.zeros((TOK, 2 * HD), jnp.float32)
            else:
                acc = states[pair][i]
                peak = acc[:, HD + 1:HD + 2]
            s = score(0)
            for j in range(len(chunks)):
                ahead = score(j + 1) if j + 1 < len(chunks) else None
                new_peak = jnp.maximum(peak, jnp.max(s, axis=1, keepdims=True))
                factor = jnp.exp2(peak - new_peak)
                weights = jnp.exp2(s - new_peak).astype(jnp.bfloat16)
                acc = acc * factor + jnp.dot(
                    weights, vx[starts[j]:starts[j] + chunks[j], :], preferred_element_type=jnp.float32)
                peak = new_peak
                s = ahead
            if not last:
                outs[0][pair * 2 + i] = jnp.where(wide == HD + 1, peak, acc)
            else:
                mass = acc[:, HD:HD + 1]
                result = (acc[:, :HD] / mass).astype(jnp.bfloat16)
                logs = peak + jnp.log2(mass)
                out = outs[pair * 2 + i]
                for k in range(4):
                    out[k, :QUARTER, :] = result[k * QUARTER:(k + 1) * QUARTER, :]
                    row = to_row(logs[k * QUARTER:(k + 1) * QUARTER, :])
                    high = row.astype(jnp.bfloat16).astype(jnp.float32)
                    mid = (row - high).astype(jnp.bfloat16).astype(jnp.float32)
                    low = row - high - mid
                    sub = lax.broadcasted_iota(jnp.int32, (ROWS - QUARTER, 128), 0)
                    tile = jnp.where(sub == 0, high, jnp.where(sub == 1, mid, jnp.where(sub == 2, low, 0.0)))
                    out[k, QUARTER:, :] = tile.astype(jnp.bfloat16)

        for i in range(2):
            block(i)


def attend(pairs, pieces, states, chunks, last):
    total = sum(p.shape[0] for p in pieces)
    assert sum(chunks) == total
    n = len(pairs)
    first = states is None
    if last:
        out = [jax.ShapeDtypeStruct((4, ROWS, HD), jnp.bfloat16)] * (2 * n)
    else:
        out = [jax.ShapeDtypeStruct((2 * n, TOK, 2 * HD), jnp.float32)]
    args = list(pairs) + list(pieces) + ([] if first else list(states))

    def kernel(*refs):
        attend_kernel(n, len(pieces), chunks, first, last, *refs)

    return pl.pallas_call(
        kernel,
        in_specs=[pl.BlockSpec(memory_space=pltpu.VMEM)] * len(args),
        out_specs=[pl.BlockSpec(memory_space=pltpu.VMEM)] * len(out),
        out_shape=out,
        scratch_shapes=[
            pltpu.VMEM((total, 2 * HD), jnp.bfloat16),
            pltpu.VMEM((total, 2 * HD), jnp.bfloat16),
        ],
        compiler_params=pltpu.CompilerParams(vmem_limit_bytes=30 * MIB),
        cost_estimate=pl.CostEstimate(
            flops=16 * n * TOK * total * HD, bytes_accessed=total * 512 + n * TOK * 2048,
            transcendentals=2 * n * TOK * total),
        name="attend",
    )(*args)


def combine_kernel(p0, p1, p2, p3, chosen, place, keep, give):
    parts = (p0, p1, p2, p3)
    core = lax.rem(place[0], 2)
    for k in range(4):
        logs = []
        for part in parts:
            tile = part[k, QUARTER:, :].astype(jnp.float32)
            logs.append(tile[0:1, :] + tile[1:2, :] + tile[2:3, :])
        top = jnp.maximum(jnp.maximum(logs[0], logs[1]), jnp.maximum(logs[2], logs[3]))
        shares = [jnp.exp2(x - top) for x in logs]
        whole = shares[0] + shares[1] + shares[2] + shares[3]
        acc = jnp.zeros((QUARTER, HD), jnp.float32)
        for share, part in zip(shares, parts):
            acc += to_column(share / whole) * part[k, :QUARTER, :].astype(jnp.float32)
        picked = to_column(chosen[k:k + 1, :].astype(jnp.float32)) > 0.5
        value = jnp.where(picked, acc, 0.0).astype(jnp.bfloat16)

        @pl.when(core == k % 2)
        def _():
            keep[k // 2] = value

        @pl.when(core != k % 2)
        def _():
            give[k // 2] = value


def combine(parts, chosen, place):
    half = jax.ShapeDtypeStruct((2, QUARTER, HD), jnp.bfloat16)
    return pl.pallas_call(
        combine_kernel,
        in_specs=[pl.BlockSpec(memory_space=pltpu.VMEM)] * 5 + [pl.BlockSpec(memory_space=pltpu.SMEM)],
        out_specs=[pl.BlockSpec(memory_space=pltpu.VMEM)] * 2,
        out_shape=[half, half],
        compiler_params=pltpu.CompilerParams(vmem_limit_bytes=16 * MIB),
        cost_estimate=pl.CostEstimate(flops=4_000_000, bytes_accessed=800_000, transcendentals=8192),
        name="combine",
    )(*parts, chosen, place)


def choose_kernel(keep, got, place, mine, theirs):
    high = lax.div(place[0], 2)
    mine[0] = keep[high]
    mine[1] = got[high]
    theirs[0] = keep[1 - high]
    theirs[1] = got[1 - high]


def choose(keep, got, place):
    half = jax.ShapeDtypeStruct((2, QUARTER, HD), jnp.bfloat16)
    return pl.pallas_call(
        choose_kernel,
        in_specs=[pl.BlockSpec(memory_space=pltpu.VMEM)] * 2 + [pl.BlockSpec(memory_space=pltpu.SMEM)],
        out_specs=[pl.BlockSpec(memory_space=pltpu.VMEM)] * 2,
        out_shape=[half, half],
        compiler_params=pltpu.CompilerParams(vmem_limit_bytes=16 * MIB),
        cost_estimate=pl.CostEstimate(flops=0, bytes_accessed=300_000, transcendentals=0),
        name="choose",
    )(keep, got, place)


def finish_kernel(mine, theirs, place, w, out, mixed):
    @pl.when(pl.program_id(0) == 0)
    def _():
        for slot, ref in ((0, mine), (2, theirs)):
            for j in range(2):
                head = lax.bitwise_xor(place[0], slot + j)
                mixed[:, pl.ds(pl.multiple_of(head * HD, HD), HD)] = ref[j]

    out[...] = jnp.dot(mixed[...], w[...], preferred_element_type=jnp.float32).astype(jnp.bfloat16)


def finish(mine, theirs, w_out, place):
    width = w_out.shape[1]
    size = 2560
    return pl.pallas_call(
        finish_kernel,
        grid=(width // size,),
        in_specs=[
            pl.BlockSpec((2, QUARTER, HD), lambda j: (0, 0, 0)),
            pl.BlockSpec((2, QUARTER, HD), lambda j: (0, 0, 0)),
            pl.BlockSpec(memory_space=pltpu.SMEM),
            pl.BlockSpec((4 * HD, size), lambda j: (0, j)),
        ],
        out_specs=pl.BlockSpec((QUARTER, size), lambda j: (0, j)),
        out_shape=jax.ShapeDtypeStruct((QUARTER, width), jnp.bfloat16),
        scratch_shapes=[pltpu.VMEM((QUARTER, 4 * HD), jnp.bfloat16)],
        compiler_params=pltpu.CompilerParams(vmem_limit_bytes=16 * MIB),
        cost_estimate=pl.CostEstimate(flops=2 * QUARTER * 4 * HD * width, bytes_accessed=7_000_000, transcendentals=0),
        name="finish",
    )(mine, theirs, place, w_out)


def shift(x, axis, by):
    return lax.ppermute(x, axis, [(i, (i + by) % 4) for i in range(4)])


def swap(x, axis, by):
    return lax.ppermute(x, axis, [(i, i ^ by) for i in range(4)])


def body(hidden, w_query, w_key, w_value, w_out, valid, window, frame_ids):
    chosen = jnp.any(frame_ids[:, None] == window[None, :], axis=1) & (valid > 0)
    chosen = chosen.astype(jnp.int32).reshape(4, QUARTER)
    h = TOK // 2
    kv = project_keys_values(hidden, w_key, w_value, valid)
    x1, x3, y1, y3 = shift(kv, "x", 1), shift(kv, "x", 3), shift(kv, "y", 1), shift(kv, "y", 3)
    late, _ = lax.optimization_barrier((hidden, kv))
    q = project_queries(late, w_query)
    near = jnp.concatenate([q, swap(q, "zh", 1)], axis=0)
    v1 = shift(jnp.concatenate([x1[:h], x3[:h], y1[:h]], axis=0), "y", 1)
    v3 = shift(jnp.concatenate([x1[:h], x3[:h], y3[h:]], axis=0), "y", 3)
    u1 = shift(jnp.concatenate([y1[h:], y3[h:], x1[:h]], axis=0), "x", 1)
    u3 = shift(jnp.concatenate([y1[h:], y3[h:], x3[h:]], axis=0), "x", 3)
    far = swap(near, "zh", 3)
    (state,) = attend([near], [kv, x1, x3, y1, y3], None, (1280, 1280), False)
    opposite = [(i * 4 + j, ((i + 2) % 4) * 4 + (j + 2) % 4) for i in range(4) for j in range(4)]
    corner = lax.ppermute(kv, ("y", "x"), opposite)
    s1 = shift(jnp.concatenate([v1[:h], v3[:h]], axis=0), "x", 1)
    s3 = shift(u3[:2 * h], "x", 3)
    t1 = shift(jnp.concatenate([u1[:h], u3[:h]], axis=0), "y", 1)
    t3 = shift(v3[:2 * h], "y", 3)
    (state_far,) = attend(
        [far], [kv, x1, x3, y1, y3, u1, u3, v1, v3], None, (1280, 1280, 1536, 1536), False)
    (state,) = attend([near], [u1, u3, v1, v3], [state], (1536, 1536), False)
    rest = [s1, s3, t1, t3, corner]
    o3, o2 = attend([far], rest, [state_far], (1280, 1280), True)
    o2, o3 = swap(o2, "zh", 2), swap(o3, "zh", 3)
    o0, o1 = attend([near], rest, [state], (1280, 1280), True)
    o1 = swap(o1, "zh", 1)
    place = lax.axis_index("head").astype(jnp.int32).reshape(1)
    keep, give = combine([o0, o1, o2, o3], chosen, place)
    got = swap(give, "head", 1)
    mine, theirs = choose(keep, got, place)
    return finish(mine, swap(theirs, "head", 2), w_out, place)


def solution(mesh):
    wide = Mesh(mesh.devices.reshape(4, 4, 4, 4), ("y", "zh", "x", "head"))
    seq = ("y", "zh", "x")
    return jax.shard_map(
        body,
        mesh=wide,
        in_specs=(
            P(seq, None),
            P(None, "head"),
            P(None, "head"),
            P(None, "head"),
            P(),
            P(seq),
            P(),
            P(seq),
        ),
        out_specs=P(seq + ("head",), None),
        check_vma=False,
    )
```
